32 devices in a mesh: dp: 8 (over z, y), tensor: 4 (over x, core).
Axes of the slice: x: 2, y: 2, z: 4, core: 2. Of those that a mesh axis runs over, the one named last changes fastest.
Arguments:
- acts: bfloat16 [4096, 8192], P('dp'), may hold values from -6 to 6
- grads_out: bfloat16 [4096, 14336], P('dp', 'tensor'), may hold values from -0.09375 to 0.09375
- kept_cols: int32 [128, 96], P(None, 'tensor'), may hold values from 0 to 56, as said below
- row_old: float32 [8192], P('dp'), may hold values from 0.05 to 1.8, as said below
- prior_column_moments: float32 [14336], P('tensor'), may hold values from 0.05 to 0.5
Outputs:
- update: bfloat16 [128, 96, 4096], P('dp', 'tensor')
- row_new: float32 [8192], P('dp')
- col_new: float32 [14336], P('tensor')
The draws below stay inside these ranges and needn't reach their ends.
Inputs may be any that keep to these rules, and one draw needn't show every extreme that they name: `kept_cols`: live entries of a block row within one index of tensor strictly increase along the slots and precede the empty value 56; each block row keeps 24 // 2 to 24 blocks in each index of tensor, and for each index of tensor some block row keeps exactly 24. `row_old`: Positive.
All inputs are finite; a program needn't handle non-finite values.
Results may differ from the reference program's by a relative error of at most 0.0004.
Values may be sent and summed in bfloat16 or wider, within the bound.
A program may use at most 256 MiB of HBM per device.

```python
import math
import jax
import jax.numpy as jnp
from jax import lax

D = 8192
FFW = 14336
TOKEN_TOTAL = 4096
NBR = 128
NBC_LOC = 56
KC = 24
N_TENSOR = 4


def draw_kept_cols(key, part):
    count_key, row_key, perm_key = jax.random.split(key, 3)
    counts = jax.random.randint(count_key, (NBR, N_TENSOR), KC // 2, KC + 1)
    forced = jax.random.randint(row_key, (N_TENSOR,), 0, NBR)
    counts = jnp.where(jnp.arange(NBR)[:, None] == forced[None, :], KC, counts)
    perm_keys = jax.random.split(perm_key, NBR * N_TENSOR)
    shuffled = jax.vmap(lambda single: jax.random.permutation(single, NBC_LOC))(perm_keys)
    shuffled = shuffled.reshape(NBR, N_TENSOR, NBC_LOC)
    slot_index = jnp.arange(NBC_LOC)
    chosen = jnp.where(slot_index[None, None, :] < counts[:, :, None], shuffled, NBC_LOC)
    chosen = jnp.sort(chosen, axis=-1)[:, :, :KC]
    return chosen.reshape(NBR, N_TENSOR * KC).astype(jnp.int32)


def draw_row_old(key, part):
    position = jnp.arange(D, dtype=jnp.float32) / D
    increasing_order = jnp.power(jnp.float32(3.0), position)
    base = jnp.exp(jax.random.uniform(key, (D,), jnp.float32, math.log(0.05), math.log(0.6)))
    return (base * increasing_order).astype(jnp.float32)


def strengthened(entries, key, source, target, blocks, factor):
    owner, partner = [(jnp.arange(entries.shape[axis_at]) // (entries.shape[axis_at] // blocks)).reshape([-1 if axis == axis_at else 1 for axis in range(entries.ndim)]) for axis_at in (source, target)]
    chosen = jax.random.permutation(key, blocks)[partner]
    strong = (owner == chosen) | (owner == (partner + blocks // 2) % blocks)
    return jnp.where(strong, factor * entries, entries)


def shard_levels(own_key, dims, cuts, least, largest):
    def one(dim, blocks):
        draws = jax.random.uniform(jax.random.fold_in(jax.random.fold_in(own_key, 6), dim), (blocks,), jnp.float32, least / len(cuts), largest / len(cuts))
        return jnp.repeat(jnp.exp(draws), dims[dim] // blocks).reshape((-1,) + (1,) * (len(dims) - dim - 1))

    level = one(*cuts[0])
    for cut in cuts[1:]:
        level = level * one(*cut)
    return level


def scatter_about(own_key, shape, spread, most, pieces=(), held_as=jnp.bfloat16):
    gain = shard_levels(own_key, shape, pieces, -0.22, 0.18) if pieces else 1.0
    array = jax.random.normal(own_key, shape, jnp.float32) * spread * gain
    return jnp.minimum(jnp.maximum(array, -most), most).astype(held_as)


def bell_draw_with(key, shape, spread, bound, cuts, heavy, kind=jnp.bfloat16):
    drawn = spread * jax.random.normal(key, shape, jnp.float32)
    if cuts:
        drawn = drawn * shard_levels(key, shape, cuts, -0.22, 0.18)
    return jnp.clip(strengthened(drawn, jax.random.fold_in(key, 3), *heavy), -bound, bound).astype(kind)


def setup_inputs(seed: int = 0) -> dict:
    key_of = jax.random.split(jax.random.key(seed), 6)
    return {
        "acts": bell_draw_with(key_of[0], (TOKEN_TOTAL, D), 1.0, 6.0, ((0, 8),), (0, 1, 8, 2.0)),
        "grads_out": scatter_about(key_of[1], (TOKEN_TOTAL, FFW), (TOKEN_TOTAL ** -0.5), 0.09375, ((0, 8), (1, 4))),
        "kept_cols": draw_kept_cols(jax.random.fold_in(key_of[5], 71), 0),
        "row_old": draw_row_old(jax.random.fold_in(key_of[5], 71), 0),
        "prior_column_moments": jnp.clip(jnp.exp(math.log(0.5) - 2.3025851 * jax.random.uniform(key_of[4], (FFW,), jnp.float32) ** shard_levels(key_of[4], (FFW,), ((0, 4),), -0.2, 0.2)), 0.05, 0.5),
    }


def reference(acts, grads_out, kept_cols, row_old, prior_column_moments):
    nbr = D // 64
    nblk = FFW // 64
    slot_count = kept_cols.shape[1]
    shard = (jnp.arange(slot_count, dtype=jnp.int32) // KC).astype(jnp.int32)
    live = kept_cols < NBC_LOC
    global_cols = jnp.where(live, kept_cols + shard[None, :] * NBC_LOC, 0).astype(jnp.int32)
    grad_blocks = grads_out.reshape(TOKEN_TOTAL, nblk, 64)

    def one_row(index):
        slab = lax.dynamic_slice_in_dim(acts, index * 64, 64, 1).astype(jnp.float32)
        selected_entries = jnp.take(grad_blocks, global_cols[index], axis=1).astype(jnp.float32)
        block = jnp.einsum('tf,tkg->kfg', slab, selected_entries, preferred_element_type=jnp.float32)
        block = jnp.where(live[index][:, None, None], block, jnp.float32(0.0))
        return block
    grad = lax.map(one_row, jnp.arange(nbr, dtype=jnp.int32))
    squared = grad * grad
    row_part = lax.optimization_barrier(jnp.sum(squared, axis=(1, 3))).reshape(D)
    row_new = 0.6 * row_old + 0.4 * row_part / FFW
    col_blocks = lax.optimization_barrier(jnp.sum(squared, axis=2)).reshape(nbr * slot_count, 64)
    col_part = jax.ops.segment_sum(col_blocks, global_cols.reshape(-1), num_segments=nblk).reshape(FFW)
    col_new = 0.6 * prior_column_moments + 0.4 * col_part / D
    mean_row = jnp.sum(row_new) / D
    row_view = row_new.reshape(nbr, 1, 64, 1)
    col_view = jnp.take(col_new.reshape(nblk, 64), global_cols, axis=0)[:, :, None, :]
    rescaled_gradient = grad * lax.rsqrt(row_view * col_view / mean_row)
    rescaled_gradient = jnp.where(live[:, :, None, None], rescaled_gradient, jnp.float32(0.0))
    update = rescaled_gradient.astype(jnp.bfloat16).reshape(nbr, slot_count, 4096)
    return (update, row_new, col_new)
```

```python
import functools

import jax
import jax.numpy as jnp
from jax import lax
from jax.experimental import pallas as pl
from jax.experimental.pallas import tpu as pltpu
from jax.sharding import PartitionSpec as P

D = 8192
FFW = 14336


def select_kernel(nblk, slots, kept_ref, w_ref, rr_ref, cc_ref, out_ref, u_ref, x_ref):
    r = pl.program_id(0)
    row_scale = rr_ref[...]
    for p in range(nblk // 2):
        cols = slice(p * 128, (p + 1) * 128)
        u_ref[p] = w_ref[:, cols] * row_scale * cc_ref[:, cols]
    first = lax.broadcasted_iota(jnp.int32, (32, 128), 1) < 64

    for k in range(slots):
        c = kept_ref[r, k]
        safe = jnp.minimum(c, nblk - 1)
        p = safe // 2
        h = safe % 2
        even = u_ref[p, pl.ds(0, 32, stride=2), :]
        odd = u_ref[p, pl.ds(1, 32, stride=2), :]
        low = jnp.where(first, even, pltpu.roll(odd, 64, 1))
        high = jnp.where(first, pltpu.roll(even, 64, 1), odd)
        block = jnp.where(h == 0, low, high)
        x_ref[k * 32 : (k + 1) * 32, :] = jnp.where(c < nblk, block, 0.0)
    for j in range(32):
        out_ref[0, :, j * 128 : (j + 1) * 128] = x_ref[pl.ds(j, slots, stride=32), :].astype(
            jnp.bfloat16
        )


def select(kept, w, rr, cc):
    rows, slots = kept.shape
    width = w.shape[1]
    nblk = width // 64
    return pl.pallas_call(
        functools.partial(select_kernel, nblk, slots),
        out_shape=jax.ShapeDtypeStruct((rows, slots, 4096), jnp.bfloat16),
        grid_spec=pltpu.PrefetchScalarGridSpec(
            num_scalar_prefetch=1,
            grid=(rows,),
            in_specs=[
                pl.BlockSpec((64, width), lambda r, _: (r, 0)),
                pl.BlockSpec((64, 1), lambda r, _: (r, 0)),
                pl.BlockSpec((1, width), lambda r, _: (0, 0)),
            ],
            out_specs=pl.BlockSpec((1, slots, 4096), lambda r, _: (r, 0, 0)),
            scratch_shapes=[
                pltpu.VMEM((nblk // 2, 64, 128), jnp.float32),
                pltpu.VMEM((slots * 32, 128), jnp.float32),
            ],
        ),
        compiler_params=pltpu.CompilerParams(vmem_limit_bytes=32 * 1024 * 1024),
    )(kept, w, rr, cc)


def finish(w, my_kept, row_old, prior):
    rows_dev = my_kept.shape[0]
    width = w.shape[1]
    nblk = width // 64
    live = (my_kept[:, :, None] == jnp.arange(nblk, dtype=jnp.int32)).any(1)
    mask = jnp.repeat(live, 64, axis=1)[:, None, :]
    w3 = w.reshape(rows_dev, 64, width)
    squared = jnp.where(mask, w3 * w3, 0.0)
    row_part = jnp.sum(squared, axis=2).reshape(rows_dev * 64)
    col_part = jnp.sum(squared, axis=(0, 1))
    share = 0.6 * jnp.sum(row_old) / lax.axis_size("tensor") + 0.4 * jnp.sum(row_part) / FFW
    mean_row = lax.psum(share, ("dp", "tensor")) / D
    row_new = 0.6 * row_old + 0.4 * lax.psum(row_part, "tensor") / FFW
    col_new = 0.6 * prior + 0.4 * lax.psum(col_part, "dp") / D
    rr = lax.rsqrt(row_new).reshape(rows_dev * 64, 1)
    cc = (lax.rsqrt(col_new) * jnp.sqrt(mean_row)).reshape(1, width)
    return select(my_kept, w, rr, cc), row_new, col_new


def per_device(acts, grads_out, kept_cols, row_old, prior):
    n_dp, n_t = lax.axis_size("dp"), lax.axis_size("tensor")
    tokens, width = grads_out.shape
    part = tokens // n_t
    rows_dev = kept_cols.shape[0] // n_dp
    my_kept = lax.dynamic_slice_in_dim(kept_cols, lax.axis_index("dp") * rows_dev, rows_dev, 0)
    mine = lax.dynamic_slice_in_dim(acts, lax.axis_index("tensor") * part, part, 0)
    mine = lax.all_to_all(mine, "dp", split_axis=1, concat_axis=0, tiled=True)
    slab = lax.all_gather(mine, "tensor", axis=0, tiled=False)
    slab = slab.reshape(n_t, n_dp, part, rows_dev * 64).transpose(1, 0, 2, 3)
    slab = slab.reshape(n_t * n_dp * part, rows_dev * 64)
    pieces = []
    half = width // 2
    for first in range(0, width, half):
        g = lax.all_gather(grads_out[:, first : first + half], "dp", axis=0, tiled=True)
        pieces.append(
            lax.dot_general(
                slab, g, (((0,), (0,)), ((), ())), preferred_element_type=jnp.float32
            )
        )
    w = jnp.concatenate(pieces, axis=1)
    return finish(w, my_kept, row_old, prior)


def solution(mesh):
    in_specs = (P("dp", None), P("dp", "tensor"), P(None, "tensor"), P("dp"), P("tensor"))
    out_specs = (P("dp", "tensor", None), P("dp"), P("tensor"))
    return jax.shard_map(
        per_device, mesh=mesh, in_specs=in_specs, out_specs=out_specs, check_vma=False
    )
```

```python
import functools

import jax
import jax.numpy as jnp
from jax import lax
from jax.experimental import pallas as pl
from jax.experimental.pallas import tpu as pltpu
from jax.sharding import PartitionSpec as P

D = 8192
FFW = 14336


def select_kernel(nblk, slots, count, kept_ref, *refs):
    w_refs, (rr_ref, cc_ref, out_ref, u_ref, x_ref) = refs[:count], refs[count:]
    r = pl.program_id(0)
    row_scale = rr_ref[...]
    per = nblk // 2 // count
    for p in range(nblk // 2):
        cols = slice(p * 128, (p + 1) * 128)
        here = slice(p % per * 128, (p % per + 1) * 128)
        u_ref[p] = w_refs[p // per][:, here] * row_scale * cc_ref[:, cols]
    first = lax.broadcasted_iota(jnp.int32, (32, 128), 1) < 64

    for k in range(slots):
        c = kept_ref[r, k]
        safe = jnp.minimum(c, nblk - 1)
        p = safe // 2
        h = safe % 2
        even = u_ref[p, pl.ds(0, 32, stride=2), :]
        odd = u_ref[p, pl.ds(1, 32, stride=2), :]
        low = jnp.where(first, even, pltpu.roll(odd, 64, 1))
        high = jnp.where(first, pltpu.roll(even, 64, 1), odd)
        block = jnp.where(h == 0, low, high)
        x_ref[k * 32 : (k + 1) * 32, :] = jnp.where(c < nblk, block, 0.0)
    for j in range(32):
        out_ref[0, :, j * 128 : (j + 1) * 128] = x_ref[pl.ds(j, slots, stride=32), :].astype(
            jnp.bfloat16
        )


def select(kept, w, rr, cc):
    rows, slots = kept.shape
    count = len(w)
    width = cc.shape[1]
    nblk = width // 64
    return pl.pallas_call(
        functools.partial(select_kernel, nblk, slots, count),
        out_shape=jax.ShapeDtypeStruct((rows, slots, 4096), jnp.bfloat16),
        grid_spec=pltpu.PrefetchScalarGridSpec(
            num_scalar_prefetch=1,
            grid=(rows,),
            in_specs=[
                *[pl.BlockSpec((64, width // count), lambda r, _: (r, 0))] * count,
                pl.BlockSpec((64, 1), lambda r, _: (r, 0)),
                pl.BlockSpec((1, width), lambda r, _: (0, 0)),
            ],
            out_specs=pl.BlockSpec((1, slots, 4096), lambda r, _: (r, 0, 0)),
            scratch_shapes=[
                pltpu.VMEM((nblk // 2, 64, 128), jnp.float32),
                pltpu.VMEM((slots * 32, 128), jnp.float32),
            ],
        ),
        compiler_params=pltpu.CompilerParams(vmem_limit_bytes=32 * 1024 * 1024),
    )(kept, *w, rr, cc)


def finish(w, my_kept, row_old, prior):
    rows_dev = my_kept.shape[0]
    width = prior.shape[0]
    nblk = width // 64
    live = (my_kept[:, :, None] == jnp.arange(nblk, dtype=jnp.int32)).any(1)
    mask = jnp.repeat(live, 64, axis=1)[:, None, :]
    row_part, col_parts, first = 0.0, [], 0
    for piece in w:
        last = first + piece.shape[1]
        w3 = piece.reshape(rows_dev, 64, last - first)
        squared = jnp.where(mask[:, :, first:last], w3 * w3, 0.0)
        row_part = row_part + jnp.sum(squared, axis=2).reshape(rows_dev * 64)
        col_parts.append(jnp.sum(squared, axis=(0, 1)))
        first = last
    row_full = jnp.sum(exchange(lambda to: row_part, "tensor"), axis=0)
    row_new = 0.6 * row_old + 0.4 * row_full / FFW
    sums = jnp.concatenate(col_parts + [jnp.broadcast_to(jnp.sum(row_new), (128,))])
    full = jnp.sum(exchange(lambda to: sums, "dp"), axis=0)
    mean_row = full[width] / D
    col_new = 0.6 * prior + 0.4 * full[:width] / D
    rr = lax.rsqrt(row_new).reshape(rows_dev * 64, 1)
    cc = (lax.rsqrt(col_new) * jnp.sqrt(mean_row)).reshape(1, width)
    return select(my_kept, w, rr, cc), row_new, col_new


def exchange(piece_for, axis):
    n = lax.axis_size(axis)
    me = lax.axis_index(axis)
    own = piece_for(me)
    held = jnp.zeros((n,) + own.shape, own.dtype)
    held = lax.dynamic_update_index_in_dim(held, own, me, 0)
    for shift in range(1, n):
        pairs = [(i, (i + shift) % n) for i in range(n)]
        got = lax.ppermute(piece_for((me + shift) % n), axis, pairs)
        held = lax.dynamic_update_index_in_dim(held, got, (me - shift) % n, 0)
    return held


def per_device(acts, grads_out, kept_cols, row_old, prior):
    n_dp, n_t = lax.axis_size("dp"), lax.axis_size("tensor")
    tokens, width = grads_out.shape
    part = tokens // n_t
    rows_dev = kept_cols.shape[0] // n_dp
    own = rows_dev * 64
    my_kept = lax.dynamic_slice_in_dim(kept_cols, lax.axis_index("dp") * rows_dev, rows_dev, 0)
    chunk = width // 2
    gathered = [
        lax.all_gather(grads_out[:, first : first + chunk], "dp", axis=0, tiled=True) for first in range(0, width, chunk)
    ]
    start = lax.axis_index("tensor") * part
    mine = exchange(lambda to: lax.dynamic_slice(acts, (start, to * own), (part, own)), "dp")
    slab = exchange(lambda to: mine, "tensor")
    slab = slab.transpose(1, 0, 2, 3).reshape(n_dp * tokens, own)
    pieces = [
        lax.dot_general(slab, g, (((0,), (0,)), ((), ())), preferred_element_type=jnp.float32)
        for g in gathered
    ]
    return finish(pieces, my_kept, row_old, prior)


def solution(mesh):
    in_specs = (P("dp", None), P("dp", "tensor"), P(None, "tensor"), P("dp"), P("tensor"))
    out_specs = (P("dp", "tensor", None), P("dp"), P("tensor"))
    return jax.shard_map(
        per_device, mesh=mesh, in_specs=in_specs, out_specs=out_specs, check_vma=False
    )
```
